32 devices in a mesh: groups: 2 (over x), fsdp: 16 (over z, y, core).
Axes of the slice: x: 2, y: 2, z: 4, core: 2. Of those that a mesh axis runs over, the one named last changes fastest.
Arguments:
- tokens: bfloat16 [8192, 8192], P(('groups', 'fsdp')), parts along dimension 0, may hold values from -6 to 6
- token_job_index: int32 [8192, 1], P(('groups', 'fsdp')), parts along dimension 0, may hold values from 0 to 63; in each aligned block of 256 rows (0 to 255, 256 to 511, ...) at most 5 rows name the same one
- cotangent: bfloat16 [8192, 1024], P(('groups', 'fsdp')), parts along dimension 0, may hold values from -0.375 to 0.375
- frozen_value_weight: bfloat16 [8192, 1024], P('fsdp'), may hold values from -0.0625 to 0.0625
- frozen_value_bias: bfloat16 [1024], replicated, may hold values from -3 to 3
- down_factor_weight: bfloat16 [128, 8192, 128], P(('groups', 'fsdp')), parts along dimension 0, may hold values from -0.0625 to 0.0625
- up_factor_weight: bfloat16 [128, 128, 1024], P(('groups', 'fsdp')), parts along dimension 0, may hold values from -0.5 to 0.5
Outputs:
- output: bfloat16 [8192, 1024], P(('groups', 'fsdp')), parts along dimension 0
- down_factor_gradient: bfloat16 [128, 8192, 128], P(('groups', 'fsdp')), parts along dimension 0
- up_factor_gradient: bfloat16 [128, 128, 1024], P(('groups', 'fsdp')), parts along dimension 0
The draws below stay inside these ranges and needn't reach their ends.
There are 2 independent parts, one for each index of `groups`. The reference program is written for one: setup_inputs(seed, part) draws one part's arguments, and reference() takes and returns one part's arrays. A program takes and returns all parts, laid end to end along the dimension named above; an argument that names none is the same for every part. Nothing has to cross between parts.
Inputs may be any that keep to these rules, and one draw needn't show every extreme that they name: `token_job_index`: among the 256 tokens of one device no job appears more than 5 times; some job reaches 5 on some device.
All inputs are finite; a program needn't handle non-finite values.
Results may differ from the reference program's by a relative error of at most 0.0051.
Values may be sent and summed in bfloat16 or wider, within the bound.
A program may use at most 128 MiB of HBM per device.

```python
import math
import jax
import jax.numpy as jnp
import numpy as np
from jax import lax

MODEL_WIDTH = 8192
VALUE_WIDTH = 1024
ADAPTER_RANK = 128
ADAPTER_JOBS = 64
TOK_DEV = 256
JOB_TOKEN_LIMIT = 5
TOKENS = 4096
N_FSDP = 16


def levels(rng, extent, split, low, high):
    def one(dim, blocks):
        steps = jax.random.uniform(jax.random.fold_in(jax.random.fold_in(rng, 6), dim), (blocks,), jnp.float32, low / len(split), high / len(split))
        return jnp.repeat(jnp.exp(steps), extent[dim] // blocks).reshape((-1,) + (1,) * (len(extent) - dim - 1))

    factor_of = one(*split[0])
    for cut in split[1:]:
        factor_of = factor_of * one(*cut)
    return factor_of


def deal_out(stream_key, own, number, rows, amount, top, bound, slope):
    sequence = jax.random.permutation(stream_key, amount)
    heavy_load, ordinary = shares(amount, rows * top, bound, slope, True), shares(amount, rows * top, bound, slope, False)
    places = jnp.arange(amount)

    def named(sizes, turn):
        used = int((sizes > 0).sum())
        fixed = max(1, used // 4)
        passed = fixed + (places - fixed + turn * (used - fixed)) % max(1, amount - fixed)
        return jnp.zeros((amount,), jnp.int32).at[sequence[jnp.where(places < fixed, places, passed)]].set(jnp.asarray(sizes, jnp.int32))

    sizes = jnp.where(number % 4 == 0, named(heavy_load, number // 4), named(ordinary, number - number // 4 - 1))
    mixed = jax.random.permutation(jax.random.fold_in(own, 3), amount)
    source_of, receiver = mixed[0:amount // 2 * 2:2], mixed[1:amount // 2 * 2:2]
    margin = jnp.minimum(sizes[source_of] - 1, bound - sizes[receiver]) // 2
    margin = jnp.where((source_of == sequence[0]) | (receiver == sequence[0]) | (sizes[receiver] == 0), 0, jnp.maximum(margin, 0))
    passed = jax.random.randint(jax.random.fold_in(own, 4), (amount // 2,), 0, 1 << 20) % (margin + 1)
    sizes = sizes.at[source_of].add(-passed).at[receiver].add(passed)
    members = jnp.searchsorted(jnp.cumsum(sizes), jnp.arange(rows * top), side="right").astype(jnp.int32)
    listing = members.reshape(top, rows).T
    listing = listing[jax.random.permutation(jax.random.fold_in(own, 1), rows)]
    turn = jax.random.randint(jax.random.fold_in(own, 2), (rows, 1), 0, top)
    return jnp.take_along_axis(listing, (jnp.arange(top)[None, :] + turn) % top, axis=1)


def shares(amount, total, limit, skew, full):
    weights = [(1 << 20) // math.isqrt(standing ** skew) + 1 for standing in range(1, amount + 1)]
    largest = limit if full else min(limit, max(-(-total // amount), total * weights[0] // sum(weights)))
    least = 1 if total - largest >= amount - 1 else 0
    given, surplus = [largest] + [least] * (amount - 1), total - largest - least * (amount - 1)
    while surplus > 0:
        movable = [i for i in range(1, amount) if given[i] < largest] or [i for i in range(1, amount) if given[i] < limit]
        whole, remaining = sum([weights[i] for i in movable]), surplus
        for i in movable:
            addition = min(limit - given[i], max(1, remaining * weights[i] // whole), surplus)
            given[i] = given[i] + addition
            surplus = surplus - addition
    return np.array(given)


def noise(rng, shape, scale, reach, shards=(), held_as=jnp.bfloat16):
    result = jax.random.normal(rng, shape, jnp.float32) * scale
    if len(shards) > 0:
        result = levels(rng, shape, shards, -0.22, 0.18) * result
    return jnp.clip(result, min=-reach, max=reach).astype(held_as)


def setup_inputs(seed: int = 0, part: int = 0) -> dict:
    key_list = jax.random.split(jax.random.key(seed), 8)
    part_splits = jax.random.split(jax.random.fold_in(key_list[7], part), 8)
    tokens = noise(part_splits[0], (TOKENS, MODEL_WIDTH), 1.0, 6.0, ((0, 16),))
    token_job_index_keys = jax.random.split(jax.random.fold_in(part_splits[1], 1), TOKENS // TOK_DEV)
    token_job_index_turns = jax.random.permutation(jax.random.fold_in(part_splits[1], 3), TOKENS // TOK_DEV)
    token_job_index = jax.vmap(lambda own, number: deal_out(jax.random.fold_in(part_splits[1], 2), own, number, TOK_DEV, ADAPTER_JOBS, 1, JOB_TOKEN_LIMIT, 2))(token_job_index_keys, token_job_index_turns).reshape((TOKENS, 1))
    cotangent = noise(part_splits[2], (TOKENS, VALUE_WIDTH), 0.0625, 0.375, ((0, 16),))
    frozen_value_weight = noise(key_list[3], (MODEL_WIDTH, VALUE_WIDTH), MODEL_WIDTH ** -0.5, 0.0625, ((0, 16),))
    frozen_value_bias = noise(key_list[4], (VALUE_WIDTH,), 0.5, 3.0)
    down_factor_weight = noise(part_splits[5], (ADAPTER_JOBS, MODEL_WIDTH, ADAPTER_RANK), MODEL_WIDTH ** -0.5, 0.0625, ((0, 16),))
    up_factor_weight = noise(part_splits[6], (ADAPTER_JOBS, ADAPTER_RANK, VALUE_WIDTH), ADAPTER_RANK ** -0.5, 0.5, ((0, 16),))
    return dict(tokens=tokens, token_job_index=token_job_index, cotangent=cotangent, frozen_value_weight=frozen_value_weight, frozen_value_bias=frozen_value_bias, down_factor_weight=down_factor_weight, up_factor_weight=up_factor_weight)


def reference(tokens, token_job_index, cotangent, frozen_value_weight, frozen_value_bias, down_factor_weight, up_factor_weight):
    base_out = jnp.dot(tokens, frozen_value_weight, preferred_element_type=jnp.float32)
    job_list = token_job_index[:, 0].astype(jnp.int32)
    sorting = jnp.argsort(job_list, stable=True).astype(jnp.int32)
    one_hot = (job_list[:, None] == jnp.arange(ADAPTER_JOBS, dtype=jnp.int32)[None, :]).astype(jnp.int32)
    counts = jnp.sum(one_hot, axis=0).astype(jnp.int32)
    starts = (jnp.cumsum(counts) - counts).astype(jnp.int32)
    window = N_FSDP * JOB_TOKEN_LIMIT
    sorted_rows = jnp.concatenate([tokens[sorting], jnp.zeros((window, MODEL_WIDTH), tokens.dtype)], axis=0)
    sorted_grads = jnp.concatenate([cotangent[sorting], jnp.zeros((window, VALUE_WIDTH), cotangent.dtype)], axis=0)

    def per_job(token_index):
        begin = starts[token_index]
        alive_mask = jnp.arange(window, dtype=jnp.int32) < counts[token_index]
        visiting_token_rows = lax.dynamic_slice_in_dim(sorted_rows, begin, window, 0)
        visiting_token_rows = jnp.where(alive_mask[:, None], visiting_token_rows, jnp.zeros_like(visiting_token_rows))
        visiting_gradient_rows = lax.dynamic_slice_in_dim(sorted_grads, begin, window, 0)
        visiting_gradient_rows = jnp.where(alive_mask[:, None], visiting_gradient_rows, jnp.zeros_like(visiting_gradient_rows))
        hidden_input = jnp.dot(visiting_token_rows, down_factor_weight[token_index], preferred_element_type=jnp.float32).astype(jnp.bfloat16)
        adapter_update = jnp.dot(hidden_input, up_factor_weight[token_index], preferred_element_type=jnp.float32).astype(jnp.bfloat16)
        rank_space_gradient = jnp.dot(visiting_gradient_rows, up_factor_weight[token_index].T, preferred_element_type=jnp.float32).astype(jnp.bfloat16)
        up_factor_gradient = jnp.dot(hidden_input.T, visiting_gradient_rows, preferred_element_type=jnp.float32).astype(jnp.bfloat16)
        down_factor_gradient = jnp.dot(visiting_token_rows.T, rank_space_gradient, preferred_element_type=jnp.float32).astype(jnp.bfloat16)
        return adapter_update, down_factor_gradient, up_factor_gradient

    delta_blocks, down_factor_gradient, up_factor_gradient = lax.map(per_job, jnp.arange(ADAPTER_JOBS, dtype=jnp.int32))
    sorted_jobs = job_list[sorting]
    within = (jnp.arange(TOKENS, dtype=jnp.int32) - starts[sorted_jobs]).astype(jnp.int32)
    delta_sorted = delta_blocks[sorted_jobs, within]
    delta_tokens = jnp.zeros((TOKENS, VALUE_WIDTH), jnp.bfloat16).at[sorting].set(delta_sorted)
    output = (base_out + frozen_value_bias.astype(jnp.float32)[None, :] + delta_tokens.astype(jnp.float32)).astype(jnp.bfloat16)
    return output, down_factor_gradient, up_factor_gradient
```

```python
import functools

import jax
import jax.numpy as jnp
from jax import lax
from jax.experimental import pallas as pl
from jax.experimental.pallas import tpu as pltpu
from jax.sharding import PartitionSpec as P

ADAPTER_JOBS = 64
JOB_TOKEN_LIMIT = 5
MESH = pl.DeviceIdType.MESH
BF16 = jnp.bfloat16
F32 = jnp.float32

ROWS = 16
FOLD = 4


def plain_body(
    tokens,
    token_job_index,
    cotangent,
    frozen_value_weight,
    frozen_value_bias,
    down_factor_weight,
    up_factor_weight,
):
    row_count = tokens.shape[0]
    device_job_index = down_factor_weight.shape[0]
    devices = lax.axis_size("fsdp")
    job_list = token_job_index[:, 0]
    one_hot = (job_list[:, None] == jnp.arange(ADAPTER_JOBS, dtype=jnp.int32)[None, :]).astype(
        jnp.int32
    )
    earlier = jnp.cumsum(one_hot, axis=0) - one_hot
    slot_in = jnp.sum(earlier * one_hot, axis=1)
    target = job_list * JOB_TOKEN_LIMIT + slot_in
    matches = (
        target[None, :] == jnp.arange(ADAPTER_JOBS * JOB_TOKEN_LIMIT, dtype=jnp.int32)[:, None]
    )
    filled = jnp.any(matches, axis=1)
    source = jnp.sum(
        matches.astype(jnp.int32) * jnp.arange(row_count, dtype=jnp.int32)[None, :], axis=1
    )
    sent_rows = jnp.where(filled[:, None], tokens[source], jnp.zeros((), tokens.dtype))
    sent_rows = sent_rows.reshape(devices, device_job_index, JOB_TOKEN_LIMIT, tokens.shape[1])
    sent_grads = jnp.where(filled[:, None], cotangent[source], jnp.zeros((), cotangent.dtype))
    sent_grads = sent_grads.reshape(devices, device_job_index, JOB_TOKEN_LIMIT, cotangent.shape[1])
    local_token_rows = lax.all_to_all(sent_rows, "fsdp", split_axis=0, concat_axis=2, tiled=True)
    local_token_rows = local_token_rows[0]
    hidden_input = jnp.einsum(
        "ypk,ykv->ypv", local_token_rows, down_factor_weight, preferred_element_type=jnp.float32
    ).astype(jnp.bfloat16)
    adapter_update = jnp.einsum(
        "ewg,egf->ewf", hidden_input, up_factor_weight, preferred_element_type=jnp.float32
    ).astype(jnp.bfloat16)
    returned_output = lax.all_to_all(
        adapter_update[None], "fsdp", split_axis=2, concat_axis=0, tiled=True
    )
    returned_output = returned_output.reshape(
        ADAPTER_JOBS * JOB_TOKEN_LIMIT, adapter_update.shape[2]
    )
    delta_tokens = returned_output[target]
    local_gradient_rows = lax.all_to_all(
        sent_grads, "fsdp", split_axis=0, concat_axis=2, tiled=True
    )
    local_gradient_rows = local_gradient_rows[0]
    rank_space_gradient = jnp.einsum(
        "buz,bhz->buh", local_gradient_rows, up_factor_weight, preferred_element_type=jnp.float32
    ).astype(jnp.bfloat16)
    up_factor_gradient = jnp.einsum(
        "jtr,jtk->jrk", hidden_input, local_gradient_rows, preferred_element_type=jnp.float32
    ).astype(jnp.bfloat16)
    down_factor_gradient = jnp.einsum(
        "jtd,jtr->jdr", local_token_rows, rank_space_gradient, preferred_element_type=jnp.float32
    ).astype(jnp.bfloat16)
    base_out = jnp.dot(
        tokens,
        lax.all_gather(frozen_value_weight, "fsdp", axis=0, tiled=True),
        preferred_element_type=jnp.float32,
    )
    output = (
        base_out + frozen_value_bias.astype(jnp.float32)[None, :] + delta_tokens.astype(jnp.float32)
    ).astype(jnp.bfloat16)
    return (output, down_factor_gradient, up_factor_gradient)


def iota(shape, dim):
    return lax.broadcasted_iota(jnp.int32, shape, dim)


def dot(a, b, dims=((1,), (0,)), precision=None):
    return lax.dot_general(a, b, (dims, ((), ())), precision=precision, preferred_element_type=F32)


def exchange_kernel(
    nz,
    tok_hbm,
    job_ref,
    cot_hbm,
    w_hbm,
    bias_ref,
    d_hbm,
    u_hbm,
    out_ref,
    r_hbm,
    gl_ref,
    glx_ref,
    h_ref,
    hx_ref,
    tok,
    cot,
    down,
    up,
    weight,
    sent,
    got,
    back,
    returned,
    pick,
    pickx,
    base,
    hidden,
    load_sem,
    a_send,
    a_recv,
    b_send,
    b_recv,
    zu_send,
    zu_recv,
    zd_send,
    zd_recv,
    y_send,
    y_recv,
    x_send,
    x_recv,
    c_send,
    c_recv,
):
    g = lax.axis_index("groups")
    f = lax.axis_index("fsdp")
    z, y, c = f // 4, (f // 2) % 2, f % 2
    count, width = tok.shape
    value = cot.shape[1]
    jobs = down.shape[0]
    rank = down.shape[2]
    depth = w_hbm.shape[0]
    half = depth // 2
    quarter = width // FOLD
    vquarter = value // FOLD
    rows = 4 * nz * ROWS
    v0 = width + quarter

    def place(zz, yy, cc):
        return zz * 4 + yy * 2 + cc

    offsets = [
        (oz, oy, oc)
        for oz in (2, 1, 3, 0)
        for oy in (1, 0)
        for oc in (0, 1)
        if (oz, oy, oc) != (0, 0, 0)
    ]

    def peer(o, sign):
        return place((z + sign * o[0] + nz) % nz, (y + o[1]) % 2, (c + o[2]) % 2)

    barrier = pltpu.get_barrier_semaphore()
    for o in offsets:
        pl.semaphore_signal(barrier, inc=1, device_id=(g, peer(o, 1)), device_id_type=MESH)
    pl.semaphore_signal(barrier, inc=1, device_id=(1 - g, f), device_id_type=MESH)

    own_rows = pl.ds(pl.multiple_of(f * depth, depth), depth)
    loads = [
        pltpu.make_async_copy(tok_hbm, tok, load_sem.at[0]),
        pltpu.make_async_copy(cot_hbm, cot, load_sem.at[1]),
        pltpu.make_async_copy(w_hbm, weight.at[own_rows, :], load_sem.at[2]),
        pltpu.make_async_copy(d_hbm, down, load_sem.at[3]),
        pltpu.make_async_copy(u_hbm, up, load_sem.at[4]),
    ]
    for load in (loads[2], loads[0], loads[1], loads[3], loads[4]):
        load.start()

    job = job_ref[...]
    mine = jnp.where(iota((ADAPTER_JOBS, count), 0) == job, 1.0, 0.0)
    before = jnp.where(iota((count, count), 0) < iota((count, count), 1), 1.0, 0.0).astype(BF16)
    earlier = dot(mine.astype(BF16), before)
    slot = jnp.sum(earlier * mine, axis=0, keepdims=True).astype(jnp.int32)
    slot = (job % jobs) * JOB_TOKEN_LIMIT + slot
    first = (job // jobs) * ROWS
    full = slot < ROWS
    row = jnp.where(full, first + slot, -rows)
    rowx = jnp.where(full, -rows, first + slot - ROWS)
    line = iota((rows, count), 0)
    pick[...] = jnp.where(line == row, 1.0, 0.0).astype(BF16)
    for k in range(FOLD):
        pickx[k] = jnp.where(line == rowx + FOLD * k, 1.0, 0.0).astype(BF16)

    def unit(zz, yy, cc, hh):
        start = pl.multiple_of(place(zz, yy, cc) * depth + hh * half, half)
        return weight.at[pl.ds(start, half), :]

    def send_unit(zz, yy, cc, hh, send, recv, device):
        block = unit(zz, yy, cc, hh)
        return pltpu.make_async_remote_copy(
            src_ref=block,
            dst_ref=block,
            send_sem=send,
            recv_sem=recv,
            device_id=device,
            device_id_type=MESH,
        )

    def z_up(k):
        return send_unit(
            z - k + 1, y, c, g, zu_send.at[k], zu_recv.at[k], (g, place(z + 1, y, c))
        )

    def z_up_in(k):
        return send_unit(z - k, y, c, g, zu_send.at[k], zu_recv.at[k], (g, place(z - 1, y, c)))

    def z_down(k):
        return send_unit(
            z + k - 1, y, c, g, zd_send.at[k], zd_recv.at[k], (g, place(z - 1, y, c))
        )

    def z_down_in(k):
        return send_unit(z + k, y, c, g, zd_send.at[k], zd_recv.at[k], (g, place(z + 1, y, c)))

    def y_out(zz):
        return send_unit(zz, y, c, g, y_send.at[zz], y_recv.at[zz], (g, place(z, 1 - y, c)))

    def y_in(zz):
        return send_unit(zz, 1 - y, c, g, y_send.at[zz], y_recv.at[zz], (g, place(z, 1 - y, c)))

    def x_out(zz, yy):
        i = zz * 2 + yy
        return send_unit(zz, yy, c, g, x_send.at[i], x_recv.at[i], (1 - g, f))

    def x_in(zz, yy):
        i = zz * 2 + yy
        return send_unit(zz, yy, c, 1 - g, x_send.at[i], x_recv.at[i], (1 - g, f))

    def c_out(zz, yy, hh):
        i = (zz * 2 + yy) * 2 + hh
        return send_unit(zz, yy, c, hh, c_send.at[i], c_recv.at[i], (g, place(z, y, 1 - c)))

    def c_in(zz, yy, hh):
        i = (zz * 2 + yy) * 2 + hh
        return send_unit(zz, yy, 1 - c, hh, c_send.at[i], c_recv.at[i], (g, place(z, y, 1 - c)))

    pl.semaphore_wait(barrier, len(offsets) + 1)
    loads[2].wait()

    @pl.when(z < nz - 1)
    def _():
        z_up(1).start()

    @pl.when(z > 0)
    def _():
        z_down(1).start()

    y_out(z).start()
    c_out(z, y, g).start()
    c_out(z, y, 1 - g).start()

    loads[0].wait()
    loads[1].wait()
    sent[:, v0 : v0 + value] = dot(pick[...], cot[...]).astype(BF16)
    folded = jnp.zeros((rows, vquarter), F32)
    for k in range(FOLD):
        folded += dot(pickx[k], cot[:, k * vquarter : (k + 1) * vquarter])
    sent[:, v0 + value :] = folded.astype(BF16)
    step = quarter // 2

    @pl.loop(0, 2)
    def _(b):
        total = jnp.zeros((rows, step), F32)
        for k in range(FOLD):
            columns = pl.ds(pl.multiple_of(k * quarter + b * step, step), step)
            total += dot(pickx[k], tok[:, columns])
        sent[:, pl.ds(pl.multiple_of(width + b * step, step), step)] = total.astype(BF16)

    @pl.loop(0, width // step)
    def _(b):
        columns = pl.ds(pl.multiple_of(b * step, step), step)
        sent[:, columns] = dot(pick[...], tok[:, columns]).astype(BF16)

    def block(ff):
        return pl.ds(pl.multiple_of(ff * ROWS, ROWS), ROWS)

    def a_copy(i):
        there = peer(offsets[i], 1)
        return pltpu.make_async_remote_copy(
            src_ref=sent.at[block(there), :],
            dst_ref=got.at[block(f), :],
            send_sem=a_send.at[i],
            recv_sem=a_recv.at[i],
            device_id=(g, there),
            device_id_type=MESH,
        )

    def a_in(i):
        there = peer(offsets[i], -1)
        return pltpu.make_async_remote_copy(
            src_ref=sent.at[block(there), :],
            dst_ref=got.at[block(there), :],
            send_sem=a_send.at[i],
            recv_sem=a_recv.at[i],
            device_id=(g, there),
            device_id_type=MESH,
        )

    for i in range(len(offsets)):
        a_copy(i).start()
    got[block(f), :] = sent[block(f), :]

    def after_y(zz):
        y_in(zz).wait_recv()
        x_out(zz, 1 - y).start()
        c_out(zz, 1 - y, g).start()

    def after_z(zz):
        y_out(zz).start()
        x_out(zz, y).start()
        c_out(zz, y, g).start()

    after_y(z)
    for k in range(1, nz):

        @pl.when(z - k >= 0)
        def _():
            z_up_in(k).wait_recv()

            @pl.when(z < nz - 1)
            def _():
                z_up(k + 1).start()

            after_z(z - k)

        @pl.when(z + k <= nz - 1)
        def _():
            z_down_in(k).wait_recv()

            @pl.when(z > 0)
            def _():
                z_down(k + 1).start()

            after_z(z + k)

        @pl.when(z - k >= 0)
        def _():
            after_y(z - k)

        @pl.when(z + k <= nz - 1)
        def _():
            after_y(z + k)

    def after_x(zz, yy):
        x_in(zz, yy).wait_recv()
        c_out(zz, yy, 1 - g).start()

    after_x(z, 1 - y)
    for k in range(1, nz):
        for yy in (y, 1 - y):

            @pl.when(z - k >= 0)
            def _():
                after_x(z - k, yy)

            @pl.when(z + k <= nz - 1)
            def _():
                after_x(z + k, yy)

    for zz in range(nz):
        for yy in range(2):
            for hh in range(2):
                c_in(zz, yy, hh).wait_recv()

    base[...] = jnp.zeros_like(base)

    @pl.loop(0, width // depth)
    def _(s):
        along = pl.ds(pl.multiple_of(s * depth, depth), depth)
        base[...] += dot(tok[:, along], weight[along, :])

    loads[3].wait()
    loads[4].wait()

    for i in range(len(offsets)):
        a_in(i).wait_recv()
    keep = pltpu.make_async_copy(got, r_hbm, load_sem.at[5])
    keep.start()

    line = iota((rows, jobs * rank), 0) % ROWS
    lane_job = iota((rows, jobs * rank), 1) // rank
    of_job = (line >= lane_job * JOB_TOKEN_LIMIT) & (line < (lane_job + 1) * JOB_TOKEN_LIMIT)
    linex = iota((rows, 1), 0) % ROWS
    of_quarter = [(linex >= k * FOLD) & (linex < (k + 1) * FOLD) for k in range(FOLD)]
    ri, ci = iota((rows, rows), 0), iota((rows, rows), 1)
    same = jnp.where((ri // ROWS == ci // ROWS) & (ri % FOLD == ci % FOLD), 1.0, 0.0)

    hidden[...] = jnp.zeros_like(hidden)

    @pl.loop(0, width // step)
    def _(b):
        along = pl.ds(pl.multiple_of(b * step, step), step)
        factors = jnp.concatenate([down[j, along, :] for j in range(jobs)], axis=1)
        hidden[...] += dot(got[:, along], factors)

    folds = jnp.zeros((rows, FOLD * rank), F32)
    for b in range(2):
        factors = jnp.concatenate(
            [
                down[jobs - 1, k * quarter + b * step : k * quarter + (b + 1) * step, :]
                for k in range(FOLD)
            ],
            axis=1,
        )
        folds += dot(got[:, width + b * step : width + (b + 1) * step], factors)
    partial = jnp.zeros((rows, rank), F32)
    for k in range(FOLD):
        partial += jnp.where(of_quarter[k], folds[:, k * rank : (k + 1) * rank], 0.0)
    hx = dot(same, partial, precision=lax.Precision.HIGHEST).astype(BF16)
    hx_ref[...] = hx
    h = jnp.where(of_job, hidden[...], 0.0).astype(BF16)
    h_ref[...] = h
    back[:, :value] = dot(h, up[...]).astype(BF16)
    deltax = dot(hx, up[(jobs - 1) * rank :, :])
    folded = jnp.zeros((rows, vquarter), F32)
    for k in range(FOLD):
        folded += jnp.where(of_quarter[k], deltax[:, k * vquarter : (k + 1) * vquarter], 0.0)
    back[:, value:] = folded.astype(BF16)

    def b_copy(i):
        there = peer(offsets[i], 1)
        return pltpu.make_async_remote_copy(
            src_ref=back.at[block(there), :],
            dst_ref=returned.at[block(f), :],
            send_sem=b_send.at[i],
            recv_sem=b_recv.at[i],
            device_id=(g, there),
            device_id_type=MESH,
        )

    def b_in(i):
        there = peer(offsets[i], -1)
        return pltpu.make_async_remote_copy(
            src_ref=back.at[block(there), :],
            dst_ref=returned.at[block(there), :],
            send_sem=b_send.at[i],
            recv_sem=b_recv.at[i],
            device_id=(g, there),
            device_id_type=MESH,
        )

    for i in range(len(offsets)):
        b_copy(i).start()
    returned[block(f), :] = back[block(f), :]

    low = dot(got[:, v0 : v0 + value], up[...], ((1,), (1,)))
    gl_ref[...] = jnp.where(of_job, low, 0.0).astype(BF16)
    partial = jnp.zeros((rows, rank), F32)
    for k in range(FOLD):
        term = dot(
            got[:, v0 + value :],
            up[(jobs - 1) * rank :, k * vquarter : (k + 1) * vquarter],
            ((1,), (1,)),
        )
        partial += jnp.where(of_quarter[k], term, 0.0)
    glx_ref[...] = dot(same, partial, precision=lax.Precision.HIGHEST).astype(BF16)
    base[...] += bias_ref[...].astype(F32)

    for i in range(len(offsets)):
        a_copy(i).wait_send()
    for k in range(1, nz):

        @pl.when((z < nz - 1) & (z - k + 1 >= 0))
        def _():
            z_up(k).wait_send()

        @pl.when((z > 0) & (z + k - 1 <= nz - 1))
        def _():
            z_down(k).wait_send()

    for zz in range(nz):
        y_out(zz).wait_send()
        x_out(zz, 1 - y).wait_send()

        @pl.when(zz != z)
        def _():
            x_out(zz, y).wait_send()

        for yy in range(2):
            for hh in range(2):
                c_out(zz, yy, hh).wait_send()
    keep.wait()

    for i in range(len(offsets)):
        b_in(i).wait_recv()
    for k in range(FOLD):
        columns = slice(k * vquarter, (k + 1) * vquarter)
        delta = dot(pick[...], returned[:, columns], ((0,), (0,)))
        delta += dot(pickx[k], returned[:, value:], ((0,), (0,)))
        out_ref[:, columns] = (base[:, columns] + delta).astype(BF16)
    for i in range(len(offsets)):
        b_copy(i).wait_send()


def gradient_kernel(per_quarter, r_ref, x_ref, v_ref, gl_ref, glx_ref, h_ref, hx_ref, dg_ref, ug_ref):
    b = pl.program_id(0)
    jobs, rank = dg_ref.shape[0], dg_ref.shape[2]
    value = ug_ref.shape[2]
    vquarter = value // FOLD
    rows = r_ref.shape[0]
    linex = iota((rows, rank), 0) % ROWS // FOLD
    zero = jnp.zeros((rows, rank), BF16)
    both = ((0,), (0,))
    for j in range(jobs):
        term = dot(r_ref[...], gl_ref[:, j * rank : (j + 1) * rank], both)
        if j == jobs - 1:
            glx = jnp.where(linex == b // per_quarter, glx_ref[...], zero)
            term += dot(x_ref[...], glx, both)
        dg_ref[j] = term.astype(BF16)

    @pl.when(b == 0)
    def _():
        for j in range(jobs):
            for k in range(FOLD):
                columns = slice(k * vquarter, (k + 1) * vquarter)
                term = dot(h_ref[:, j * rank : (j + 1) * rank], v_ref[:, columns], both)
                if j == jobs - 1:
                    hx = jnp.where(linex == k, hx_ref[...], zero)
                    term += dot(hx, v_ref[:, value:], both)
                ug_ref[j, :, columns] = term.astype(BF16)


def fused_body(
    nz,
    tokens,
    token_job_index,
    cotangent,
    frozen_value_weight,
    frozen_value_bias,
    down_factor_weight,
    up_factor_weight,
):
    count, width = tokens.shape
    value = cotangent.shape[1]
    jobs, _, rank = down_factor_weight.shape
    n = 4 * nz
    rows = n * ROWS
    quarter, vquarter = width // FOLD, value // FOLD
    packed = width + quarter + value + vquarter
    anywhere = pl.BlockSpec(memory_space=pl.ANY)
    vmem = pl.BlockSpec(memory_space=pltpu.VMEM)
    dma = pltpu.SemaphoreType.DMA
    output, rows_in, gl, glx, h, hx = pl.pallas_call(
        functools.partial(exchange_kernel, nz),
        out_shape=(
            jax.ShapeDtypeStruct((count, value), BF16),
            jax.ShapeDtypeStruct((rows, packed), BF16),
            jax.ShapeDtypeStruct((rows, jobs * rank), BF16),
            jax.ShapeDtypeStruct((rows, rank), BF16),
            jax.ShapeDtypeStruct((rows, jobs * rank), BF16),
            jax.ShapeDtypeStruct((rows, rank), BF16),
        ),
        in_specs=[anywhere, vmem, anywhere, anywhere, vmem, anywhere, anywhere],
        out_specs=(vmem, anywhere, vmem, vmem, vmem, vmem),
        scratch_shapes=[
            pltpu.VMEM((count, width), BF16),
            pltpu.VMEM((count, value), BF16),
            pltpu.VMEM((jobs, width, rank), BF16),
            pltpu.VMEM((jobs * rank, value), BF16),
            pltpu.VMEM((width, value), BF16),
            pltpu.VMEM((rows, packed), BF16),
            pltpu.VMEM((rows, packed), BF16),
            pltpu.VMEM((rows, value + vquarter), BF16),
            pltpu.VMEM((rows, value + vquarter), BF16),
            pltpu.VMEM((rows, count), BF16),
            pltpu.VMEM((FOLD, rows, count), BF16),
            pltpu.VMEM((count, value), F32),
            pltpu.VMEM((rows, jobs * rank), F32),
            dma((6,)),
            dma((n - 1,)),
            dma((n - 1,)),
            dma((n - 1,)),
            dma((n - 1,)),
            dma((nz + 1,)),
            dma((nz + 1,)),
            dma((nz + 1,)),
            dma((nz + 1,)),
            dma((nz,)),
            dma((nz,)),
            dma((2 * nz,)),
            dma((2 * nz,)),
            dma((4 * nz,)),
            dma((4 * nz,)),
        ],
        compiler_params=pltpu.CompilerParams(
            collective_id=0, has_side_effects=True, vmem_limit_bytes=58 * 1024 * 1024
        ),
        name="exchange",
    )(
        tokens,
        token_job_index.reshape(1, count),
        cotangent,
        frozen_value_weight,
        frozen_value_bias.reshape(1, value),
        down_factor_weight,
        up_factor_weight.reshape(jobs * rank, value),
    )
    step = quarter // 2
    whole = lambda shape: pl.BlockSpec(shape, lambda b: (0,) * len(shape))
    down_gradient, up_gradient = pl.pallas_call(
        functools.partial(gradient_kernel, 2),
        grid=(width // step,),
        out_shape=(
            jax.ShapeDtypeStruct((jobs, width, rank), BF16),
            jax.ShapeDtypeStruct((jobs, rank, value), BF16),
        ),
        in_specs=[
            pl.BlockSpec((rows, step), lambda b: (0, b)),
            pl.BlockSpec((rows, step), lambda b: (0, width // step + b % 2)),
            pl.BlockSpec(
                (rows, value + vquarter), lambda b: (0, (width + quarter) // (value + vquarter))
            ),
            whole((rows, jobs * rank)),
            whole((rows, rank)),
            whole((rows, jobs * rank)),
            whole((rows, rank)),
        ],
        out_specs=(
            pl.BlockSpec((jobs, step, rank), lambda b: (0, b, 0)),
            whole((jobs, rank, value)),
        ),
        compiler_params=pltpu.CompilerParams(vmem_limit_bytes=32 * 1024 * 1024),
        name="gradients",
    )(rows_in, rows_in, rows_in, gl, glx, h, hx)
    return output, down_gradient, up_gradient


def solution(mesh):
    groups, n = mesh.shape["groups"], mesh.shape["fsdp"]
    fused = groups == 2 and n * 4 == ADAPTER_JOBS
    body = functools.partial(fused_body, n // 4) if fused else plain_body
    return jax.shard_map(
        body,
        mesh=mesh,
        in_specs=(
            P(("groups", "fsdp"), None),
            P(("groups", "fsdp"), None),
            P(("groups", "fsdp"), None),
            P("fsdp", None),
            P(),
            P(("groups", "fsdp"), None, None),
            P(("groups", "fsdp"), None, None),
        ),
        out_specs=(
            P(("groups", "fsdp"), None),
            P(("groups", "fsdp"), None, None),
            P(("groups", "fsdp"), None, None),
        ),
        check_vma=False,
    )
```

```python
import functools

import jax
import jax.numpy as jnp
from jax import lax
from jax.experimental import pallas as pl
from jax.experimental.pallas import tpu as pltpu
from jax.sharding import PartitionSpec as P

ADAPTER_JOBS = 64
JOB_TOKEN_LIMIT = 5
MESH = pl.DeviceIdType.MESH
BF16 = jnp.bfloat16
F32 = jnp.float32

ROWS = 16
FOLD = 4
PIECES = 1
WINDOW = 15
SPACING = 1


def plain_body(
    tokens,
    token_job_index,
    cotangent,
    frozen_value_weight,
    frozen_value_bias,
    down_factor_weight,
    up_factor_weight,
):
    row_count = tokens.shape[0]
    device_job_index = down_factor_weight.shape[0]
    devices = lax.axis_size("fsdp")
    job_list = token_job_index[:, 0]
    one_hot = (job_list[:, None] == jnp.arange(ADAPTER_JOBS, dtype=jnp.int32)[None, :]).astype(
        jnp.int32
    )
    earlier = jnp.cumsum(one_hot, axis=0) - one_hot
    slot_in = jnp.sum(earlier * one_hot, axis=1)
    target = job_list * JOB_TOKEN_LIMIT + slot_in
    matches = (
        target[None, :] == jnp.arange(ADAPTER_JOBS * JOB_TOKEN_LIMIT, dtype=jnp.int32)[:, None]
    )
    filled = jnp.any(matches, axis=1)
    source = jnp.sum(
        matches.astype(jnp.int32) * jnp.arange(row_count, dtype=jnp.int32)[None, :], axis=1
    )
    sent_rows = jnp.where(filled[:, None], tokens[source], jnp.zeros((), tokens.dtype))
    sent_rows = sent_rows.reshape(devices, device_job_index, JOB_TOKEN_LIMIT, tokens.shape[1])
    sent_grads = jnp.where(filled[:, None], cotangent[source], jnp.zeros((), cotangent.dtype))
    sent_grads = sent_grads.reshape(devices, device_job_index, JOB_TOKEN_LIMIT, cotangent.shape[1])
    local_token_rows = lax.all_to_all(sent_rows, "fsdp", split_axis=0, concat_axis=2, tiled=True)
    local_token_rows = local_token_rows[0]
    hidden_input = jnp.einsum(
        "ypk,ykv->ypv", local_token_rows, down_factor_weight, preferred_element_type=jnp.float32
    ).astype(jnp.bfloat16)
    adapter_update = jnp.einsum(
        "ewg,egf->ewf", hidden_input, up_factor_weight, preferred_element_type=jnp.float32
    ).astype(jnp.bfloat16)
    returned_output = lax.all_to_all(
        adapter_update[None], "fsdp", split_axis=2, concat_axis=0, tiled=True
    )
    returned_output = returned_output.reshape(
        ADAPTER_JOBS * JOB_TOKEN_LIMIT, adapter_update.shape[2]
    )
    delta_tokens = returned_output[target]
    local_gradient_rows = lax.all_to_all(
        sent_grads, "fsdp", split_axis=0, concat_axis=2, tiled=True
    )
    local_gradient_rows = local_gradient_rows[0]
    rank_space_gradient = jnp.einsum(
        "buz,bhz->buh", local_gradient_rows, up_factor_weight, preferred_element_type=jnp.float32
    ).astype(jnp.bfloat16)
    up_factor_gradient = jnp.einsum(
        "jtr,jtk->jrk", hidden_input, local_gradient_rows, preferred_element_type=jnp.float32
    ).astype(jnp.bfloat16)
    down_factor_gradient = jnp.einsum(
        "jtd,jtr->jdr", local_token_rows, rank_space_gradient, preferred_element_type=jnp.float32
    ).astype(jnp.bfloat16)
    base_out = jnp.dot(
        tokens,
        lax.all_gather(frozen_value_weight, "fsdp", axis=0, tiled=True),
        preferred_element_type=jnp.float32,
    )
    output = (
        base_out + frozen_value_bias.astype(jnp.float32)[None, :] + delta_tokens.astype(jnp.float32)
    ).astype(jnp.bfloat16)
    return (output, down_factor_gradient, up_factor_gradient)


def iota(shape, dim):
    return lax.broadcasted_iota(jnp.int32, shape, dim)


def dot(a, b, dims=((1,), (0,)), precision=None):
    return lax.dot_general(a, b, (dims, ((), ())), precision=precision, preferred_element_type=F32)


def exchange_kernel(
    nz,
    tok_hbm,
    job_ref,
    cot_hbm,
    w_hbm,
    bias_ref,
    d_hbm,
    u_hbm,
    out_ref,
    r_hbm,
    side_ref,
    tok,
    cot,
    down,
    up,
    weight,
    sent,
    got,
    back,
    returned,
    pick,
    pickx,
    base,
    hidden,
    load_sem,
    a_send,
    a_recv,
    b_send,
    b_recv,
    zu_send,
    zu_recv,
    zd_send,
    zd_recv,
    y_send,
    y_recv,
    x_send,
    x_recv,
    c_send,
    c_recv,
):
    g = lax.axis_index("groups")
    f = lax.axis_index("fsdp")
    z, y, c = f // 4, (f // 2) % 2, f % 2
    count, width = tok.shape
    value = cot.shape[1]
    jobs = down.shape[0]
    rank = down.shape[2]
    depth = w_hbm.shape[0]
    half = depth // 2
    quarter = width // FOLD
    vquarter = value // FOLD
    rows = 4 * nz * ROWS
    v0 = width + quarter

    def place(zz, yy, cc):
        return zz * 4 + yy * 2 + cc

    offsets = [
        (oz, oy, oc)
        for oz in (2, 1, 3, 0)
        for oy in (1, 0)
        for oc in (0, 1)
        if (oz, oy, oc) != (0, 0, 0)
    ]

    def peer(o, sign):
        return place((z + sign * o[0] + nz) % nz, (y + o[1]) % 2, (c + o[2]) % 2)

    barrier = pltpu.get_barrier_semaphore()
    for o in offsets:
        pl.semaphore_signal(barrier, inc=1, device_id=(g, peer(o, 1)), device_id_type=MESH)
    pl.semaphore_signal(barrier, inc=1, device_id=(1 - g, f), device_id_type=MESH)

    own_rows = pl.ds(pl.multiple_of(f * depth, depth), depth)
    loads = [
        pltpu.make_async_copy(tok_hbm, tok, load_sem.at[0]),
        pltpu.make_async_copy(cot_hbm, cot, load_sem.at[1]),
        pltpu.make_async_copy(w_hbm, weight.at[own_rows, :], load_sem.at[2]),
        pltpu.make_async_copy(d_hbm, down, load_sem.at[3]),
        pltpu.make_async_copy(u_hbm, up, load_sem.at[4]),
    ]
    for load in (loads[2], loads[0], loads[1], loads[3], loads[4]):
        load.start()

    job = job_ref[...]
    mine = jnp.where(iota((ADAPTER_JOBS, count), 0) == job, 1.0, 0.0)
    before = jnp.where(iota((count, count), 0) < iota((count, count), 1), 1.0, 0.0).astype(BF16)
    earlier = dot(mine.astype(BF16), before)
    slot = jnp.sum(earlier * mine, axis=0, keepdims=True).astype(jnp.int32)
    slot = (job % jobs) * JOB_TOKEN_LIMIT + slot
    first = (job // jobs) * ROWS
    full = slot < ROWS
    row = jnp.where(full, first + slot, -rows)
    rowx = jnp.where(full, -rows, first + slot - ROWS)
    line = iota((rows, count), 0)
    pick[...] = jnp.where(line == row, 1.0, 0.0).astype(BF16)
    for k in range(FOLD):
        pickx[k] = jnp.where(line == rowx + FOLD * k, 1.0, 0.0).astype(BF16)

    def unit(zz, yy, cc, hh):
        start = pl.multiple_of(place(zz, yy, cc) * depth + hh * half, half)
        return weight.at[pl.ds(start, half), :]

    def send_unit(zz, yy, cc, hh, send, recv, device):
        block = unit(zz, yy, cc, hh)
        return pltpu.make_async_remote_copy(
            src_ref=block,
            dst_ref=block,
            send_sem=send,
            recv_sem=recv,
            device_id=device,
            device_id_type=MESH,
        )

    def z_up(k):
        return send_unit(
            z - k + 1, y, c, g, zu_send.at[k], zu_recv.at[k], (g, place(z + 1, y, c))
        )

    def z_up_in(k):
        return send_unit(z - k, y, c, g, zu_send.at[k], zu_recv.at[k], (g, place(z - 1, y, c)))

    def z_down(k):
        return send_unit(
            z + k - 1, y, c, g, zd_send.at[k], zd_recv.at[k], (g, place(z - 1, y, c))
        )

    def z_down_in(k):
        return send_unit(z + k, y, c, g, zd_send.at[k], zd_recv.at[k], (g, place(z + 1, y, c)))

    def y_out(zz):
        return send_unit(zz, y, c, g, y_send.at[zz], y_recv.at[zz], (g, place(z, 1 - y, c)))

    def y_in(zz):
        return send_unit(zz, 1 - y, c, g, y_send.at[zz], y_recv.at[zz], (g, place(z, 1 - y, c)))

    def x_out(zz, yy):
        i = zz * 2 + yy
        return send_unit(zz, yy, c, g, x_send.at[i], x_recv.at[i], (1 - g, f))

    def x_in(zz, yy):
        i = zz * 2 + yy
        return send_unit(zz, yy, c, 1 - g, x_send.at[i], x_recv.at[i], (1 - g, f))

    def c_out(zz, yy, hh):
        i = (zz * 2 + yy) * 2 + hh
        return send_unit(zz, yy, c, hh, c_send.at[i], c_recv.at[i], (g, place(z, y, 1 - c)))

    def c_in(zz, yy, hh):
        i = (zz * 2 + yy) * 2 + hh
        return send_unit(zz, yy, 1 - c, hh, c_send.at[i], c_recv.at[i], (g, place(z, y, 1 - c)))

    pl.semaphore_wait(barrier, len(offsets) + 1)
    loads[2].wait()

    @pl.when(z < nz - 1)
    def _():
        z_up(1).start()

    @pl.when(z > 0)
    def _():
        z_down(1).start()

    y_out(z).start()
    c_out(z, y, g).start()
    c_out(z, y, 1 - g).start()

    loads[0].wait()
    loads[1].wait()
    sent[:, v0 : v0 + value] = dot(pick[...], cot[...]).astype(BF16)
    folded = jnp.zeros((rows, vquarter), F32)
    for k in range(FOLD):
        folded += dot(pickx[k], cot[:, k * vquarter : (k + 1) * vquarter])
    sent[:, v0 + value :] = folded.astype(BF16)
    step = quarter // 2

    @pl.loop(0, 2)
    def _(b):
        total = jnp.zeros((rows, step), F32)
        for k in range(FOLD):
            columns = pl.ds(pl.multiple_of(k * quarter + b * step, step), step)
            total += dot(pickx[k], tok[:, columns])
        sent[:, pl.ds(pl.multiple_of(width + b * step, step), step)] = total.astype(BF16)

    @pl.loop(0, width // step)
    def _(b):
        columns = pl.ds(pl.multiple_of(b * step, step), step)
        sent[:, columns] = dot(pick[...], tok[:, columns]).astype(BF16)

    def block(ff):
        return pl.ds(pl.multiple_of(ff * ROWS, ROWS), ROWS)

    strip = sent.shape[1] // PIECES
    pieces = [(i, p) for p in range(PIECES) for i in range(len(offsets))]

    def a_copy(q):
        i, p = pieces[q]
        there = peer(offsets[i], 1)
        columns = pl.ds(p * strip, strip)
        return pltpu.make_async_remote_copy(
            src_ref=sent.at[block(there), columns],
            dst_ref=got.at[block(f), columns],
            send_sem=a_send.at[q],
            recv_sem=a_recv.at[q],
            device_id=(g, there),
            device_id_type=MESH,
        )

    def a_in(q):
        i, p = pieces[q]
        there = peer(offsets[i], -1)
        columns = pl.ds(p * strip, strip)
        return pltpu.make_async_remote_copy(
            src_ref=sent.at[block(there), columns],
            dst_ref=got.at[block(there), columns],
            send_sem=a_send.at[q],
            recv_sem=a_recv.at[q],
            device_id=(g, there),
            device_id_type=MESH,
        )

    got[block(f), :] = sent[block(f), :]

    def after_y(zz):
        y_in(zz).wait_recv()
        x_out(zz, 1 - y).start()
        c_out(zz, 1 - y, g).start()

    def after_z(zz):
        y_out(zz).start()
        x_out(zz, y).start()
        c_out(zz, y, g).start()

    def after_x(zz, yy):
        x_in(zz, yy).wait_recv()
        c_out(zz, yy, 1 - g).start()

    def either(k, act):
        @pl.when(z - k >= 0)
        def _():
            act(z - k)

        @pl.when(z + k <= nz - 1)
        def _():
            act(z + k)

    def relay_z(k):
        @pl.when(z - k >= 0)
        def _():
            z_up_in(k).wait_recv()

            @pl.when(z < nz - 1)
            def _():
                z_up(k + 1).start()

            after_z(z - k)

        @pl.when(z + k <= nz - 1)
        def _():
            z_down_in(k).wait_recv()

            @pl.when(z > 0)
            def _():
                z_down(k + 1).start()

            after_z(z + k)

    relay_z(1)
    relays = [lambda: after_y(z)]
    for k in range(1, nz):
        if k > 1:
            relays.append(functools.partial(relay_z, k))
        relays.append(functools.partial(either, k, after_y))
    relays.append(lambda: after_x(z, 1 - y))
    for k in range(1, nz):
        relays.append(functools.partial(either, k, lambda zz: after_x(zz, y)))
        relays.append(functools.partial(either, k, lambda zz: after_x(zz, 1 - y)))

    for q in range(WINDOW):
        a_copy(q).start()
    for q in range(len(pieces)):
        a_copy(q).wait_send()
        if q + WINDOW < len(pieces):
            a_copy(q + WINDOW).start()
        if q % SPACING == SPACING - 1 and relays:
            relays.pop(0)()
    for relay in relays:
        relay()

    loads[3].wait()
    loads[4].wait()

    for q in range(len(pieces)):
        a_in(q).wait_recv()
    keep = pltpu.make_async_copy(got, r_hbm, load_sem.at[5])
    keep.start()

    line = iota((rows, jobs * rank), 0) % ROWS
    lane_job = iota((rows, jobs * rank), 1) // rank
    of_job = (line >= lane_job * JOB_TOKEN_LIMIT) & (line < (lane_job + 1) * JOB_TOKEN_LIMIT)
    linex = iota((rows, 1), 0) % ROWS
    of_quarter = [(linex >= k * FOLD) & (linex < (k + 1) * FOLD) for k in range(FOLD)]
    ri, ci = iota((rows, rows), 0), iota((rows, rows), 1)
    same = jnp.where((ri // ROWS == ci // ROWS) & (ri % FOLD == ci % FOLD), 1.0, 0.0)

    hidden[...] = jnp.zeros_like(hidden)

    @pl.loop(0, width // step)
    def _(b):
        along = pl.ds(pl.multiple_of(b * step, step), step)
        factors = jnp.concatenate([down[j, along, :] for j in range(jobs)], axis=1)
        hidden[...] += dot(got[:, along], factors)

    folds = jnp.zeros((rows, FOLD * rank), F32)
    for b in range(2):
        factors = jnp.concatenate(
            [
                down[jobs - 1, k * quarter + b * step : k * quarter + (b + 1) * step, :]
                for k in range(FOLD)
            ],
            axis=1,
        )
        folds += dot(got[:, width + b * step : width + (b + 1) * step], factors)
    partial = jnp.zeros((rows, rank), F32)
    for k in range(FOLD):
        partial += jnp.where(of_quarter[k], folds[:, k * rank : (k + 1) * rank], 0.0)
    hx = dot(same, partial, precision=lax.Precision.HIGHEST).astype(BF16)
    side_ref[:, 2 * jobs * rank + rank :] = hx
    h = jnp.where(of_job, hidden[...], 0.0).astype(BF16)
    side_ref[:, jobs * rank : 2 * jobs * rank] = h
    back[:, :value] = dot(h, up[...]).astype(BF16)
    deltax = dot(hx, up[(jobs - 1) * rank :, :])
    folded = jnp.zeros((rows, vquarter), F32)
    for k in range(FOLD):
        folded += jnp.where(of_quarter[k], deltax[:, k * vquarter : (k + 1) * vquarter], 0.0)
    back[:, value:] = folded.astype(BF16)

    def b_copy(i):
        there = peer(offsets[i], 1)
        return pltpu.make_async_remote_copy(
            src_ref=back.at[block(there), :],
            dst_ref=returned.at[block(f), :],
            send_sem=b_send.at[i],
            recv_sem=b_recv.at[i],
            device_id=(g, there),
            device_id_type=MESH,
        )

    def b_in(i):
        there = peer(offsets[i], -1)
        return pltpu.make_async_remote_copy(
            src_ref=back.at[block(there), :],
            dst_ref=returned.at[block(there), :],
            send_sem=b_send.at[i],
            recv_sem=b_recv.at[i],
            device_id=(g, there),
            device_id_type=MESH,
        )

    for i in range(len(offsets)):
        b_copy(i).start()
    returned[block(f), :] = back[block(f), :]

    low = dot(got[:, v0 : v0 + value], up[...], ((1,), (1,)))
    side_ref[:, : jobs * rank] = jnp.where(of_job, low, 0.0).astype(BF16)
    partial = jnp.zeros((rows, rank), F32)
    for k in range(FOLD):
        term = dot(
            got[:, v0 + value :],
            up[(jobs - 1) * rank :, k * vquarter : (k + 1) * vquarter],
            ((1,), (1,)),
        )
        partial += jnp.where(of_quarter[k], term, 0.0)
    glx = dot(same, partial, precision=lax.Precision.HIGHEST).astype(BF16)
    side_ref[:, 2 * jobs * rank : 2 * jobs * rank + rank] = glx

    for zz in range(nz):
        for yy in range(2):
            for hh in range(2):
                c_in(zz, yy, hh).wait_recv()
    base[...] = jnp.zeros_like(base) + bias_ref[...].astype(F32)

    @pl.loop(0, width // depth)
    def _(s):
        along = pl.ds(pl.multiple_of(s * depth, depth), depth)
        base[...] += dot(tok[:, along], weight[along, :])


    for k in range(1, nz):

        @pl.when((z < nz - 1) & (z - k + 1 >= 0))
        def _():
            z_up(k).wait_send()

        @pl.when((z > 0) & (z + k - 1 <= nz - 1))
        def _():
            z_down(k).wait_send()

    for zz in range(nz):
        y_out(zz).wait_send()
        x_out(zz, 1 - y).wait_send()

        @pl.when(zz != z)
        def _():
            x_out(zz, y).wait_send()

        for yy in range(2):
            for hh in range(2):
                c_out(zz, yy, hh).wait_send()
    keep.wait()

    for i in range(len(offsets)):
        b_in(i).wait_recv()
    for k in range(FOLD):
        columns = slice(k * vquarter, (k + 1) * vquarter)
        delta = dot(pick[...], returned[:, columns], ((0,), (0,)))
        delta += dot(pickx[k], returned[:, value:], ((0,), (0,)))
        out_ref[:, columns] = (base[:, columns] + delta).astype(BF16)
    for i in range(len(offsets)):
        b_copy(i).wait_send()


def gradient_kernel(per_quarter, r_ref, x_ref, v_ref, side_ref, dg_ref, ug_ref):
    b = pl.program_id(0)
    jobs, rank = dg_ref.shape[0], dg_ref.shape[2]
    value = ug_ref.shape[2]
    vquarter = value // FOLD
    rows = r_ref.shape[0]
    wide = jobs * rank
    linex = iota((rows, rank), 0) % ROWS // FOLD
    zero = jnp.zeros((rows, rank), BF16)
    both = ((0,), (0,))
    terms = dot(r_ref[...], side_ref[:, :wide], both)
    glx = jnp.where(linex == b // per_quarter, side_ref[:, 2 * wide : 2 * wide + rank], zero)
    folded = dot(x_ref[...], glx, both)
    for j in range(jobs):
        term = terms[:, j * rank : (j + 1) * rank]
        if j == jobs - 1:
            term += folded
        dg_ref[j] = term.astype(BF16)

    @pl.when(b == 0)
    def _():
        terms = dot(side_ref[:, wide : 2 * wide], v_ref[:, :value], both)
        for k in range(FOLD):
            columns = slice(k * vquarter, (k + 1) * vquarter)
            hx = jnp.where(linex == k, side_ref[:, 2 * wide + rank :], zero)
            folded = dot(hx, v_ref[:, value:], both)
            for j in range(jobs):
                term = terms[j * rank : (j + 1) * rank, columns]
                if j == jobs - 1:
                    term += folded
                ug_ref[j, :, columns] = term.astype(BF16)


def fused_body(
    nz,
    tokens,
    token_job_index,
    cotangent,
    frozen_value_weight,
    frozen_value_bias,
    down_factor_weight,
    up_factor_weight,
):
    count, width = tokens.shape
    value = cotangent.shape[1]
    jobs, _, rank = down_factor_weight.shape
    n = 4 * nz
    rows = n * ROWS
    quarter, vquarter = width // FOLD, value // FOLD
    packed = width + quarter + value + vquarter
    anywhere = pl.BlockSpec(memory_space=pl.ANY)
    vmem = pl.BlockSpec(memory_space=pltpu.VMEM)
    dma = pltpu.SemaphoreType.DMA
    output, rows_in, side = pl.pallas_call(
        functools.partial(exchange_kernel, nz),
        out_shape=(
            jax.ShapeDtypeStruct((count, value), BF16),
            jax.ShapeDtypeStruct((rows, packed), BF16),
            jax.ShapeDtypeStruct((rows, 2 * (jobs + 1) * rank), BF16),
        ),
        in_specs=[anywhere, vmem, anywhere, anywhere, vmem, anywhere, anywhere],
        out_specs=(vmem, anywhere, vmem),
        scratch_shapes=[
            pltpu.VMEM((count, width), BF16),
            pltpu.VMEM((count, value), BF16),
            pltpu.VMEM((jobs, width, rank), BF16),
            pltpu.VMEM((jobs * rank, value), BF16),
            pltpu.VMEM((width, value), BF16),
            pltpu.VMEM((rows, packed), BF16),
            pltpu.VMEM((rows, packed), BF16),
            pltpu.VMEM((rows, value + vquarter), BF16),
            pltpu.VMEM((rows, value + vquarter), BF16),
            pltpu.VMEM((rows, count), BF16),
            pltpu.VMEM((FOLD, rows, count), BF16),
            pltpu.VMEM((count, value), F32),
            pltpu.VMEM((rows, jobs * rank), F32),
            dma((6,)),
            dma((PIECES * (n - 1),)),
            dma((PIECES * (n - 1),)),
            dma((n - 1,)),
            dma((n - 1,)),
            dma((nz + 1,)),
            dma((nz + 1,)),
            dma((nz + 1,)),
            dma((nz + 1,)),
            dma((nz,)),
            dma((nz,)),
            dma((2 * nz,)),
            dma((2 * nz,)),
            dma((4 * nz,)),
            dma((4 * nz,)),
        ],
        compiler_params=pltpu.CompilerParams(
            collective_id=0, has_side_effects=True, vmem_limit_bytes=58 * 1024 * 1024
        ),
        name="exchange",
    )(
        tokens,
        token_job_index.reshape(1, count),
        cotangent,
        frozen_value_weight,
        frozen_value_bias.reshape(1, value),
        down_factor_weight,
        up_factor_weight.reshape(jobs * rank, value),
    )
    step = quarter // 2
    whole = lambda shape: pl.BlockSpec(shape, lambda b: (0,) * len(shape))
    down_gradient, up_gradient = pl.pallas_call(
        functools.partial(gradient_kernel, 2),
        grid=(width // step,),
        out_shape=(
            jax.ShapeDtypeStruct((jobs, width, rank), BF16),
            jax.ShapeDtypeStruct((jobs, rank, value), BF16),
        ),
        in_specs=[
            pl.BlockSpec((rows, step), lambda b: (0, b)),
            pl.BlockSpec((rows, step), lambda b: (0, width // step + b % 2)),
            pl.BlockSpec(
                (rows, value + vquarter), lambda b: (0, (width + quarter) // (value + vquarter))
            ),
            whole((rows, 2 * (jobs + 1) * rank)),
        ],
        out_specs=(
            pl.BlockSpec((jobs, step, rank), lambda b: (0, b, 0)),
            whole((jobs, rank, value)),
        ),
        compiler_params=pltpu.CompilerParams(vmem_limit_bytes=58 * 1024 * 1024),
        name="gradients",
    )(rows_in, rows_in, rows_in, side)
    return output, down_gradient, up_gradient


def solution(mesh):
    groups, n = mesh.shape["groups"], mesh.shape["fsdp"]
    fused = groups == 2 and n * 4 == ADAPTER_JOBS
    body = functools.partial(fused_body, n // 4) if fused else plain_body
    return jax.shard_map(
        body,
        mesh=mesh,
        in_specs=(
            P(("groups", "fsdp"), None),
            P(("groups", "fsdp"), None),
            P(("groups", "fsdp"), None),
            P("fsdp", None),
            P(),
            P(("groups", "fsdp"), None, None),
            P(("groups", "fsdp"), None, None),
        ),
        out_specs=(
            P(("groups", "fsdp"), None),
            P(("groups", "fsdp"), None, None),
            P(("groups", "fsdp"), None, None),
        ),
        check_vma=False,
    )
```

```python
import functools

import jax
import jax.numpy as jnp
from jax import lax
from jax.experimental import pallas as pl
from jax.experimental.pallas import tpu as pltpu
from jax.sharding import PartitionSpec as P

ADAPTER_JOBS = 64
JOB_TOKEN_LIMIT = 5
MESH = pl.DeviceIdType.MESH
BF16 = jnp.bfloat16
F32 = jnp.float32

ROWS = 16
FOLD = 4
PIECES = 1
WINDOW = 15
SPACING = 1


def plain_body(
    tokens,
    token_job_index,
    cotangent,
    frozen_value_weight,
    frozen_value_bias,
    down_factor_weight,
    up_factor_weight,
):
    row_count = tokens.shape[0]
    device_job_index = down_factor_weight.shape[0]
    devices = lax.axis_size("fsdp")
    job_list = token_job_index[:, 0]
    one_hot = (job_list[:, None] == jnp.arange(ADAPTER_JOBS, dtype=jnp.int32)[None, :]).astype(
        jnp.int32
    )
    earlier = jnp.cumsum(one_hot, axis=0) - one_hot
    slot_in = jnp.sum(earlier * one_hot, axis=1)
    target = job_list * JOB_TOKEN_LIMIT + slot_in
    matches = (
        target[None, :] == jnp.arange(ADAPTER_JOBS * JOB_TOKEN_LIMIT, dtype=jnp.int32)[:, None]
    )
    filled = jnp.any(matches, axis=1)
    source = jnp.sum(
        matches.astype(jnp.int32) * jnp.arange(row_count, dtype=jnp.int32)[None, :], axis=1
    )
    sent_rows = jnp.where(filled[:, None], tokens[source], jnp.zeros((), tokens.dtype))
    sent_rows = sent_rows.reshape(devices, device_job_index, JOB_TOKEN_LIMIT, tokens.shape[1])
    sent_grads = jnp.where(filled[:, None], cotangent[source], jnp.zeros((), cotangent.dtype))
    sent_grads = sent_grads.reshape(devices, device_job_index, JOB_TOKEN_LIMIT, cotangent.shape[1])
    local_token_rows = lax.all_to_all(sent_rows, "fsdp", split_axis=0, concat_axis=2, tiled=True)
    local_token_rows = local_token_rows[0]
    hidden_input = jnp.einsum(
        "ypk,ykv->ypv", local_token_rows, down_factor_weight, preferred_element_type=jnp.float32
    ).astype(jnp.bfloat16)
    adapter_update = jnp.einsum(
        "ewg,egf->ewf", hidden_input, up_factor_weight, preferred_element_type=jnp.float32
    ).astype(jnp.bfloat16)
    returned_output = lax.all_to_all(
        adapter_update[None], "fsdp", split_axis=2, concat_axis=0, tiled=True
    )
    returned_output = returned_output.reshape(
        ADAPTER_JOBS * JOB_TOKEN_LIMIT, adapter_update.shape[2]
    )
    delta_tokens = returned_output[target]
    local_gradient_rows = lax.all_to_all(
        sent_grads, "fsdp", split_axis=0, concat_axis=2, tiled=True
    )
    local_gradient_rows = local_gradient_rows[0]
    rank_space_gradient = jnp.einsum(
        "buz,bhz->buh", local_gradient_rows, up_factor_weight, preferred_element_type=jnp.float32
    ).astype(jnp.bfloat16)
    up_factor_gradient = jnp.einsum(
        "jtr,jtk->jrk", hidden_input, local_gradient_rows, preferred_element_type=jnp.float32
    ).astype(jnp.bfloat16)
    down_factor_gradient = jnp.einsum(
        "jtd,jtr->jdr", local_token_rows, rank_space_gradient, preferred_element_type=jnp.float32
    ).astype(jnp.bfloat16)
    base_out = jnp.dot(
        tokens,
        lax.all_gather(frozen_value_weight, "fsdp", axis=0, tiled=True),
        preferred_element_type=jnp.float32,
    )
    output = (
        base_out + frozen_value_bias.astype(jnp.float32)[None, :] + delta_tokens.astype(jnp.float32)
    ).astype(jnp.bfloat16)
    return (output, down_factor_gradient, up_factor_gradient)


def iota(shape, dim):
    return lax.broadcasted_iota(jnp.int32, shape, dim)


def dot(a, b, dims=((1,), (0,)), precision=None):
    return lax.dot_general(a, b, (dims, ((), ())), precision=precision, preferred_element_type=F32)


def exchange_kernel(
    nz,
    tok_hbm,
    job_ref,
    cot_hbm,
    w_hbm,
    bias_ref,
    d_hbm,
    u_hbm,
    out_ref,
    r_hbm,
    side_ref,
    tok,
    cot,
    down,
    up,
    weight,
    sent,
    got,
    back,
    returned,
    pick,
    pickx,
    base,
    hidden,
    load_sem,
    a_send,
    a_recv,
    b_send,
    b_recv,
    zu_send,
    zu_recv,
    zd_send,
    zd_recv,
    y_send,
    y_recv,
    x_send,
    x_recv,
    c_send,
    c_recv,
):
    g = lax.axis_index("groups")
    f = lax.axis_index("fsdp")
    z, y, c = f // 4, (f // 2) % 2, f % 2
    count, width = tok.shape
    value = cot.shape[1]
    jobs = down.shape[0]
    rank = down.shape[2]
    depth = w_hbm.shape[0]
    half = depth // 2
    quarter = width // FOLD
    vquarter = value // FOLD
    rows = 4 * nz * ROWS
    v0 = width + quarter

    def place(zz, yy, cc):
        return zz * 4 + yy * 2 + cc

    offsets = [
        (oz, oy, oc)
        for oz in (2, 1, 3, 0)
        for oy in (1, 0)
        for oc in (0, 1)
        if (oz, oy, oc) != (0, 0, 0)
    ]

    def peer(o, sign):
        return place((z + sign * o[0] + nz) % nz, (y + o[1]) % 2, (c + o[2]) % 2)

    barrier = pltpu.get_barrier_semaphore()
    for o in offsets:
        pl.semaphore_signal(barrier, inc=1, device_id=(g, peer(o, 1)), device_id_type=MESH)
    pl.semaphore_signal(barrier, inc=1, device_id=(1 - g, f), device_id_type=MESH)

    own_rows = pl.ds(pl.multiple_of(f * depth, depth), depth)
    loads = [
        pltpu.make_async_copy(tok_hbm, tok, load_sem.at[0]),
        pltpu.make_async_copy(cot_hbm, cot, load_sem.at[1]),
        pltpu.make_async_copy(w_hbm, weight.at[own_rows, :], load_sem.at[2]),
        pltpu.make_async_copy(d_hbm, down, load_sem.at[3]),
        pltpu.make_async_copy(u_hbm, up, load_sem.at[4]),
    ]
    for load in (loads[2], loads[0], loads[1], loads[3], loads[4]):
        load.start()

    job = job_ref[...]
    mine = jnp.where(iota((ADAPTER_JOBS, count), 0) == job, 1.0, 0.0)
    before = jnp.where(iota((count, count), 0) < iota((count, count), 1), 1.0, 0.0).astype(BF16)
    earlier = dot(mine.astype(BF16), before)
    slot = jnp.sum(earlier * mine, axis=0, keepdims=True).astype(jnp.int32)
    slot = (job % jobs) * JOB_TOKEN_LIMIT + slot
    first = (job // jobs) * ROWS
    full = slot < ROWS
    row = jnp.where(full, first + slot, -rows)
    rowx = jnp.where(full, -rows, first + slot - ROWS)
    line = iota((rows, count), 0)
    pick[...] = jnp.where(line == row, 1.0, 0.0).astype(BF16)
    for k in range(FOLD):
        pickx[k] = jnp.where(line == rowx + FOLD * k, 1.0, 0.0).astype(BF16)

    def unit(zz, yy, cc, hh):
        start = pl.multiple_of(place(zz, yy, cc) * depth + hh * half, half)
        return weight.at[pl.ds(start, half), :]

    def send_unit(zz, yy, cc, hh, send, recv, device):
        block = unit(zz, yy, cc, hh)
        return pltpu.make_async_remote_copy(
            src_ref=block,
            dst_ref=block,
            send_sem=send,
            recv_sem=recv,
            device_id=device,
            device_id_type=MESH,
        )

    def z_up(k):
        return send_unit(
            z - k + 1, y, c, g, zu_send.at[k], zu_recv.at[k], (g, place(z + 1, y, c))
        )

    def z_up_in(k):
        return send_unit(z - k, y, c, g, zu_send.at[k], zu_recv.at[k], (g, place(z - 1, y, c)))

    def z_down(k):
        return send_unit(
            z + k - 1, y, c, g, zd_send.at[k], zd_recv.at[k], (g, place(z - 1, y, c))
        )

    def z_down_in(k):
        return send_unit(z + k, y, c, g, zd_send.at[k], zd_recv.at[k], (g, place(z + 1, y, c)))

    def y_out(zz):
        return send_unit(zz, y, c, g, y_send.at[zz], y_recv.at[zz], (g, place(z, 1 - y, c)))

    def y_in(zz):
        return send_unit(zz, 1 - y, c, g, y_send.at[zz], y_recv.at[zz], (g, place(z, 1 - y, c)))

    def x_out(zz, yy):
        i = zz * 2 + yy
        return send_unit(zz, yy, c, g, x_send.at[i], x_recv.at[i], (1 - g, f))

    def x_in(zz, yy):
        i = zz * 2 + yy
        return send_unit(zz, yy, c, 1 - g, x_send.at[i], x_recv.at[i], (1 - g, f))

    def c_out(zz, yy, hh):
        i = (zz * 2 + yy) * 2 + hh
        return send_unit(zz, yy, c, hh, c_send.at[i], c_recv.at[i], (g, place(z, y, 1 - c)))

    def c_in(zz, yy, hh):
        i = (zz * 2 + yy) * 2 + hh
        return send_unit(zz, yy, 1 - c, hh, c_send.at[i], c_recv.at[i], (g, place(z, y, 1 - c)))

    pl.semaphore_wait(barrier, len(offsets) + 1)
    loads[2].wait()

    @pl.when(z < nz - 1)
    def _():
        z_up(1).start()

    @pl.when(z > 0)
    def _():
        z_down(1).start()

    y_out(z).start()
    c_out(z, y, g).start()
    c_out(z, y, 1 - g).start()

    loads[0].wait()
    loads[1].wait()
    sent[:, v0 : v0 + value] = dot(pick[...], cot[...]).astype(BF16)
    folded = jnp.zeros((rows, vquarter), F32)
    for k in range(FOLD):
        folded += dot(pickx[k], cot[:, k * vquarter : (k + 1) * vquarter])
    sent[:, v0 + value :] = folded.astype(BF16)
    step = quarter // 2

    @pl.loop(0, 2)
    def _(b):
        total = jnp.zeros((rows, step), F32)
        for k in range(FOLD):
            columns = pl.ds(pl.multiple_of(k * quarter + b * step, step), step)
            total += dot(pickx[k], tok[:, columns])
        sent[:, pl.ds(pl.multiple_of(width + b * step, step), step)] = total.astype(BF16)

    @pl.loop(0, width // step)
    def _(b):
        columns = pl.ds(pl.multiple_of(b * step, step), step)
        sent[:, columns] = dot(pick[...], tok[:, columns]).astype(BF16)

    def block(ff):
        return pl.ds(pl.multiple_of(ff * ROWS, ROWS), ROWS)

    strip = sent.shape[1] // PIECES
    pieces = [(i, p) for p in range(PIECES) for i in range(len(offsets))]

    def a_copy(q):
        i, p = pieces[q]
        there = peer(offsets[i], 1)
        columns = pl.ds(p * strip, strip)
        return pltpu.make_async_remote_copy(
            src_ref=sent.at[block(there), columns],
            dst_ref=got.at[block(f), columns],
            send_sem=a_send.at[q],
            recv_sem=a_recv.at[q],
            device_id=(g, there),
            device_id_type=MESH,
        )

    def a_in(q):
        i, p = pieces[q]
        there = peer(offsets[i], -1)
        columns = pl.ds(p * strip, strip)
        return pltpu.make_async_remote_copy(
            src_ref=sent.at[block(there), columns],
            dst_ref=got.at[block(there), columns],
            send_sem=a_send.at[q],
            recv_sem=a_recv.at[q],
            device_id=(g, there),
            device_id_type=MESH,
        )

    got[block(f), :] = sent[block(f), :]

    def after_y(zz):
        y_in(zz).wait_recv()
        x_out(zz, 1 - y).start()
        c_out(zz, 1 - y, g).start()

    def after_z(zz):
        y_out(zz).start()
        x_out(zz, y).start()
        c_out(zz, y, g).start()

    def after_x(zz, yy):
        x_in(zz, yy).wait_recv()
        c_out(zz, yy, 1 - g).start()

    def either(k, act):
        @pl.when(z - k >= 0)
        def _():
            act(z - k)

        @pl.when(z + k <= nz - 1)
        def _():
            act(z + k)

    def relay_z(k):
        @pl.when(z - k >= 0)
        def _():
            z_up_in(k).wait_recv()

            @pl.when(z < nz - 1)
            def _():
                z_up(k + 1).start()

            after_z(z - k)

        @pl.when(z + k <= nz - 1)
        def _():
            z_down_in(k).wait_recv()

            @pl.when(z > 0)
            def _():
                z_down(k + 1).start()

            after_z(z + k)

    relay_z(1)
    relays = [lambda: after_y(z)]
    for k in range(1, nz):
        if k > 1:
            relays.append(functools.partial(relay_z, k))
        relays.append(functools.partial(either, k, after_y))
    relays.append(lambda: after_x(z, 1 - y))
    for k in range(1, nz):
        relays.append(functools.partial(either, k, lambda zz: after_x(zz, y)))
        relays.append(functools.partial(either, k, lambda zz: after_x(zz, 1 - y)))

    for q in range(WINDOW):
        a_copy(q).start()
    for q in range(len(pieces)):
        a_copy(q).wait_send()
        if q + WINDOW < len(pieces):
            a_copy(q + WINDOW).start()
        if q % SPACING == SPACING - 1 and relays:
            relays.pop(0)()
    for relay in relays:
        relay()

    loads[3].wait()
    loads[4].wait()

    for q in range(len(pieces)):
        a_in(q).wait_recv()
    keep = pltpu.make_async_copy(got, r_hbm, load_sem.at[5])
    keep.start()

    line = iota((rows, jobs * rank), 0) % ROWS
    lane_job = iota((rows, jobs * rank), 1) // rank
    of_job = (line >= lane_job * JOB_TOKEN_LIMIT) & (line < (lane_job + 1) * JOB_TOKEN_LIMIT)
    linex = iota((rows, 1), 0) % ROWS
    of_quarter = [(linex >= k * FOLD) & (linex < (k + 1) * FOLD) for k in range(FOLD)]
    ri, ci = iota((rows, rows), 0), iota((rows, rows), 1)
    same = jnp.where((ri // ROWS == ci // ROWS) & (ri % FOLD == ci % FOLD), 1.0, 0.0)

    hidden[...] = jnp.zeros_like(hidden)

    @pl.loop(0, width // step)
    def _(b):
        along = pl.ds(pl.multiple_of(b * step, step), step)
        factors = jnp.concatenate([down[j, along, :] for j in range(jobs)], axis=1)
        hidden[...] += dot(got[:, along], factors)

    folds = jnp.zeros((rows, FOLD * rank), F32)
    for b in range(2):
        factors = jnp.concatenate(
            [
                down[jobs - 1, k * quarter + b * step : k * quarter + (b + 1) * step, :]
                for k in range(FOLD)
            ],
            axis=1,
        )
        folds += dot(got[:, width + b * step : width + (b + 1) * step], factors)
    partial = jnp.zeros((rows, rank), F32)
    for k in range(FOLD):
        partial += jnp.where(of_quarter[k], folds[:, k * rank : (k + 1) * rank], 0.0)
    hx = dot(same, partial, precision=lax.Precision.HIGHEST).astype(BF16)
    side_ref[:, 2 * jobs * rank + rank :] = hx
    h = jnp.where(of_job, hidden[...], 0.0).astype(BF16)
    side_ref[:, jobs * rank : 2 * jobs * rank] = h
    back[:, :value] = dot(h, up[...]).astype(BF16)
    deltax = dot(hx, up[(jobs - 1) * rank :, :])
    folded = jnp.zeros((rows, vquarter), F32)
    for k in range(FOLD):
        folded += jnp.where(of_quarter[k], deltax[:, k * vquarter : (k + 1) * vquarter], 0.0)
    back[:, value:] = folded.astype(BF16)

    def b_copy(i):
        there = peer(offsets[i], 1)
        return pltpu.make_async_remote_copy(
            src_ref=back.at[block(there), :],
            dst_ref=returned.at[block(f), :],
            send_sem=b_send.at[i],
            recv_sem=b_recv.at[i],
            device_id=(g, there),
            device_id_type=MESH,
        )

    def b_in(i):
        there = peer(offsets[i], -1)
        return pltpu.make_async_remote_copy(
            src_ref=back.at[block(there), :],
            dst_ref=returned.at[block(there), :],
            send_sem=b_send.at[i],
            recv_sem=b_recv.at[i],
            device_id=(g, there),
            device_id_type=MESH,
        )

    for i in range(len(offsets)):
        b_copy(i).start()
    returned[block(f), :] = back[block(f), :]

    low = dot(got[:, v0 : v0 + value], up[...], ((1,), (1,)))
    side_ref[:, : jobs * rank] = jnp.where(of_job, low, 0.0).astype(BF16)
    partial = jnp.zeros((rows, rank), F32)
    for k in range(FOLD):
        term = dot(
            got[:, v0 + value :],
            up[(jobs - 1) * rank :, k * vquarter : (k + 1) * vquarter],
            ((1,), (1,)),
        )
        partial += jnp.where(of_quarter[k], term, 0.0)
    glx = dot(same, partial, precision=lax.Precision.HIGHEST).astype(BF16)
    side_ref[:, 2 * jobs * rank : 2 * jobs * rank + rank] = glx

    for zz in range(nz):
        for yy in range(2):
            for hh in range(2):
                c_in(zz, yy, hh).wait_recv()
    base[...] = jnp.zeros_like(base) + bias_ref[...].astype(F32)

    @pl.loop(0, width // depth)
    def _(s):
        along = pl.ds(pl.multiple_of(s * depth, depth), depth)
        base[...] += dot(tok[:, along], weight[along, :])


    for k in range(1, nz):

        @pl.when((z < nz - 1) & (z - k + 1 >= 0))
        def _():
            z_up(k).wait_send()

        @pl.when((z > 0) & (z + k - 1 <= nz - 1))
        def _():
            z_down(k).wait_send()

    for zz in range(nz):
        y_out(zz).wait_send()
        x_out(zz, 1 - y).wait_send()

        @pl.when(zz != z)
        def _():
            x_out(zz, y).wait_send()

        for yy in range(2):
            for hh in range(2):
                c_out(zz, yy, hh).wait_send()
    keep.wait()

    for i in range(len(offsets)):
        b_in(i).wait_recv()
    for k in range(FOLD):
        columns = slice(k * vquarter, (k + 1) * vquarter)
        delta = dot(pick[...], returned[:, columns], ((0,), (0,)))
        delta += dot(pickx[k], returned[:, value:], ((0,), (0,)))
        out_ref[:, columns] = (base[:, columns] + delta).astype(BF16)
    for i in range(len(offsets)):
        b_copy(i).wait_send()


def gradient_kernel(r_hbm, side_ref, dg_hbm, ug_hbm, got, down, up, in_sem, out_sem):
    jobs, width, rank = down.shape
    value = up.shape[2]
    vquarter = value // FOLD
    rows = got.shape[0]
    wide = jobs * rank
    quarter = width // FOLD
    step = quarter // 2
    blocks = width // step
    both = ((0,), (0,))

    def load(b):
        along = slice(b * step, (b + 1) * step) if b < blocks else slice(width, got.shape[1])
        return pltpu.make_async_copy(r_hbm.at[:, along], got.at[:, along], in_sem.at[b])

    def leave(b, j):
        along = slice(b * step, (b + 1) * step)
        return pltpu.make_async_copy(
            down.at[j, along, :], dg_hbm.at[j, along, :], out_sem.at[b * jobs + j]
        )

    leave_up = pltpu.make_async_copy(up, ug_hbm, out_sem.at[blocks * jobs])
    for b in (blocks, *range(blocks)):
        load(b).start()
    linex = iota((rows, rank), 0) % ROWS // FOLD
    zero = jnp.zeros((rows, rank), BF16)
    load(blocks).wait()
    for b in range(blocks):
        load(b).wait()
        along = slice(b * step, (b + 1) * step)
        alongx = slice(width + b % 2 * step, width + (b % 2 + 1) * step)
        terms = dot(got[:, along], side_ref[:, :wide], both)
        glx = jnp.where(linex == b // 2, side_ref[:, 2 * wide : 2 * wide + rank], zero)
        folded = dot(got[:, alongx], glx, both)
        for j in range(jobs):
            term = terms[:, j * rank : (j + 1) * rank]
            if j == jobs - 1:
                term += folded
            down[j, along, :] = term.astype(BF16)
            leave(b, j).start()
    v0 = width + quarter
    terms = dot(side_ref[:, wide : 2 * wide], got[:, v0 : v0 + value], both)
    for k in range(FOLD):
        columns = slice(k * vquarter, (k + 1) * vquarter)
        hx = jnp.where(linex == k, side_ref[:, 2 * wide + rank :], zero)
        folded = dot(hx, got[:, v0 + value :], both)
        for j in range(jobs):
            term = terms[j * rank : (j + 1) * rank, columns]
            if j == jobs - 1:
                term += folded
            up[j, :, columns] = term.astype(BF16)
    leave_up.start()
    for b in range(blocks):
        for j in range(jobs):
            leave(b, j).wait()
    leave_up.wait()


def fused_body(
    nz,
    tokens,
    token_job_index,
    cotangent,
    frozen_value_weight,
    frozen_value_bias,
    down_factor_weight,
    up_factor_weight,
):
    count, width = tokens.shape
    value = cotangent.shape[1]
    jobs, _, rank = down_factor_weight.shape
    n = 4 * nz
    rows = n * ROWS
    quarter, vquarter = width // FOLD, value // FOLD
    packed = width + quarter + value + vquarter
    anywhere = pl.BlockSpec(memory_space=pl.ANY)
    vmem = pl.BlockSpec(memory_space=pltpu.VMEM)
    dma = pltpu.SemaphoreType.DMA
    output, rows_in, side = pl.pallas_call(
        functools.partial(exchange_kernel, nz),
        out_shape=(
            jax.ShapeDtypeStruct((count, value), BF16),
            jax.ShapeDtypeStruct((rows, packed), BF16),
            jax.ShapeDtypeStruct((rows, 2 * (jobs + 1) * rank), BF16),
        ),
        in_specs=[anywhere, vmem, anywhere, anywhere, vmem, anywhere, anywhere],
        out_specs=(vmem, anywhere, vmem),
        scratch_shapes=[
            pltpu.VMEM((count, width), BF16),
            pltpu.VMEM((count, value), BF16),
            pltpu.VMEM((jobs, width, rank), BF16),
            pltpu.VMEM((jobs * rank, value), BF16),
            pltpu.VMEM((width, value), BF16),
            pltpu.VMEM((rows, packed), BF16),
            pltpu.VMEM((rows, packed), BF16),
            pltpu.VMEM((rows, value + vquarter), BF16),
            pltpu.VMEM((rows, value + vquarter), BF16),
            pltpu.VMEM((rows, count), BF16),
            pltpu.VMEM((FOLD, rows, count), BF16),
            pltpu.VMEM((count, value), F32),
            pltpu.VMEM((rows, jobs * rank), F32),
            dma((6,)),
            dma((PIECES * (n - 1),)),
            dma((PIECES * (n - 1),)),
            dma((n - 1,)),
            dma((n - 1,)),
            dma((nz + 1,)),
            dma((nz + 1,)),
            dma((nz + 1,)),
            dma((nz + 1,)),
            dma((nz,)),
            dma((nz,)),
            dma((2 * nz,)),
            dma((2 * nz,)),
            dma((4 * nz,)),
            dma((4 * nz,)),
        ],
        compiler_params=pltpu.CompilerParams(
            collective_id=0, has_side_effects=True, vmem_limit_bytes=58 * 1024 * 1024
        ),
        name="exchange",
    )(
        tokens,
        token_job_index.reshape(1, count),
        cotangent,
        frozen_value_weight,
        frozen_value_bias.reshape(1, value),
        down_factor_weight,
        up_factor_weight.reshape(jobs * rank, value),
    )
    down_gradient, up_gradient = pl.pallas_call(
        gradient_kernel,
        out_shape=(
            jax.ShapeDtypeStruct((jobs, width, rank), BF16),
            jax.ShapeDtypeStruct((jobs, rank, value), BF16),
        ),
        in_specs=[anywhere, vmem],
        out_specs=(anywhere, anywhere),
        scratch_shapes=[
            pltpu.VMEM((rows, packed), BF16),
            pltpu.VMEM((jobs, width, rank), BF16),
            pltpu.VMEM((jobs, rank, value), BF16),
            dma((2 * FOLD + 1,)),
            dma((2 * FOLD * jobs + 1,)),
        ],
        compiler_params=pltpu.CompilerParams(vmem_limit_bytes=58 * 1024 * 1024),
        name="gradients",
    )(rows_in, side)
    return output, down_gradient, up_gradient


def solution(mesh):
    groups, n = mesh.shape["groups"], mesh.shape["fsdp"]
    fused = groups == 2 and n * 4 == ADAPTER_JOBS
    body = functools.partial(fused_body, n // 4) if fused else plain_body
    return jax.shard_map(
        body,
        mesh=mesh,
        in_specs=(
            P(("groups", "fsdp"), None),
            P(("groups", "fsdp"), None),
            P(("groups", "fsdp"), None),
            P("fsdp", None),
            P(),
            P(("groups", "fsdp"), None, None),
            P(("groups", "fsdp"), None, None),
        ),
        out_specs=(
            P(("groups", "fsdp"), None),
            P(("groups", "fsdp"), None, None),
            P(("groups", "fsdp"), None, None),
        ),
        check_vma=False,
    )
```
